32 devices in a mesh: groups: 2 (over x), tok: 8 (over z, y), head: 2 (over core).
Axes of the slice: x: 2, y: 2, z: 4, core: 2. Of those that a mesh axis runs over, the one named last changes fastest.
Arguments:
- video_query: bfloat16 [2, 4096, 4096], P('groups', ('tok', 'head')), parts along dimension 0, may hold values from -640 to 640
- video_key: bfloat16 [2, 4096, 4096], P('groups', ('tok', 'head')), parts along dimension 0, may hold values from -6 to 6
- video_value: bfloat16 [2, 4096, 4096], P('groups', ('tok', 'head')), parts along dimension 0, may hold values from -6 to 6
- audio_query: bfloat16 [2, 1024, 2048], P('groups', ('tok', 'head')), parts along dimension 0, may hold values from -640 to 640
- audio_key: bfloat16 [2, 1024, 2048], P('groups', ('tok', 'head')), parts along dimension 0, may hold values from -6 to 6
- audio_value: bfloat16 [2, 1024, 2048], P('groups', ('tok', 'head')), parts along dimension 0, may hold values from -6 to 6
- cross_audio_query: bfloat16 [2, 1024, 2048], P('groups', ('tok', 'head')), parts along dimension 0, may hold values from -640 to 640
- cross_video_key: bfloat16 [2, 4096, 2048], P('groups', ('tok', 'head')), parts along dimension 0, may hold values from -6 to 6
- cross_video_value: bfloat16 [2, 4096, 2048], P('groups', ('tok', 'head')), parts along dimension 0, may hold values from -6 to 6
- cross_video_query: bfloat16 [2, 4096, 2048], P('groups', ('tok', 'head')), parts along dimension 0, may hold values from -640 to 640
- cross_audio_key: bfloat16 [2, 1024, 2048], P('groups', ('tok', 'head')), parts along dimension 0, may hold values from -6 to 6
- cross_audio_value: bfloat16 [2, 1024, 2048], P('groups', ('tok', 'head')), parts along dimension 0, may hold values from -6 to 6
- audio_frames: int32 [2, 1024], P('groups', ('tok', 'head')), parts along dimension 0, may hold values from 0 to 15
- into_audio_slope: float32 [32], replicated, may hold values from 0.05 to 0.5
- into_video_slope: float32 [32], replicated, may hold values from 0.05 to 0.5
- timestep: int32 [2], P('groups'), parts along dimension 0, may hold values from 0 to 63
- video_gate: bfloat16 [64, 4096], replicated, may hold values from 2 to 12
- audio_gate: bfloat16 [64, 2048], replicated, may hold values from 2 to 12
- into_audio_gate: bfloat16 [64, 2048], replicated, may hold values from 2 to 12
- into_video_gate: bfloat16 [64, 2048], replicated, may hold values from 2 to 12
Outputs:
- video_self: bfloat16 [2, 4096, 4096], P('groups', ('tok', 'head')), parts along dimension 0
- audio_self: bfloat16 [2, 1024, 2048], P('groups', ('tok', 'head')), parts along dimension 0
- audio_cross: bfloat16 [2, 1024, 2048], P('groups', ('tok', 'head')), parts along dimension 0
- video_cross: bfloat16 [2, 4096, 2048], P('groups', ('tok', 'head')), parts along dimension 0
The draws below stay inside these ranges and needn't reach their ends.
There are 2 independent parts, one for each index of `groups`. The reference program is written for one: setup_inputs(seed, part) draws one part's arguments, and reference() takes and returns one part's arrays. A program takes and returns all parts, laid end to end along the dimension named above; an argument that names none is the same for every part. Nothing has to cross between parts.
All inputs are finite; a program needn't handle non-finite values.
Results may differ from the reference program's by a relative error of at most 0.0075.
Values may be sent and summed in bfloat16 or wider, within the bound.
A program may use at most 128 MiB of HBM per device.

```python
import math
import jax
import jax.numpy as jnp
from jax import lax

SAMPLES = 1
LV = 4096
LA = 1024
FRAMES = 16
HV = 32
DHV = 128
HA = 32
DHA = 64
TSTEPS = 64
DV = 4096
DA = 2048


def paired_draw(key, query_count, key_count, heads_n, head_width, salt):
    folded = jax.random.fold_in(key, salt)
    streams = jax.random.split(folded, 2)
    columns = heads_n * head_width
    queries = jnp.clip(jax.random.normal(streams[0], (SAMPLES, query_count, columns), jnp.float32), -6.0, 6.0)
    keyed = 1.5 * jax.random.truncated_normal(streams[1], -4.0, 4.0, (SAMPLES, key_count, columns), jnp.float32)
    return (queries, keyed)


def draw_video_query(key, part):
    return paired_draw(key, LV, LV, HV, DHV, 11)[0].astype(jnp.bfloat16)


def draw_video_key(key, part):
    return paired_draw(key, LV, LV, HV, DHV, 11)[1].astype(jnp.bfloat16)


def draw_audio_query(key, part):
    return paired_draw(key, LA, LA, HA, DHA, 12)[0].astype(jnp.bfloat16)


def draw_audio_key(key, part):
    return paired_draw(key, LA, LA, HA, DHA, 12)[1].astype(jnp.bfloat16)


def draw_cross_audio_query(key, part):
    return paired_draw(key, LA, LV, HA, DHA, 13)[0].astype(jnp.bfloat16)


def draw_cross_video_key(key, part):
    return paired_draw(key, LA, LV, HA, DHA, 13)[1].astype(jnp.bfloat16)


def draw_cross_video_query(key, part):
    return paired_draw(key, LV, LA, HA, DHA, 14)[0].astype(jnp.bfloat16)


def draw_cross_audio_key(key, part):
    return paired_draw(key, LV, LA, HA, DHA, 14)[1].astype(jnp.bfloat16)


def place_ends(values, stream_key, low, high):
    longest = values.shape.index(max(values.shape))
    spots = []
    for shift in (0, 1):
        where = [jax.random.randint(jax.random.fold_in(stream_key, axis), (), 0, length) for axis, length in enumerate(values.shape)]
        where[longest] = (where[longest] + shift) % values.shape[longest]
        spots.append(tuple(where))
    return values.at[spots[0]].set(low).at[spots[1]].set(high)


def shard_levels(own_key, extent, pieces, least, largest):
    gain, own = 1.0, jax.random.fold_in(own_key, 6)
    for axis_at, blocks in pieces:
        draws = jnp.exp(jax.random.uniform(jax.random.fold_in(own, axis_at), (blocks,), jnp.float32, least / len(pieces), largest / len(pieces)))
        gain = gain * jnp.repeat(draws, extent[axis_at] // blocks).reshape([-1 if axis == axis_at else 1 for axis in range(len(extent))])
    return gain


def centred(own_key, extent, scale, bound, cuts=(), held_as=jnp.bfloat16):
    factor_of = shard_levels(own_key, extent, cuts, -0.22, 0.18) if cuts else 1.0
    entries = jax.random.normal(own_key, extent, jnp.float32) * scale * factor_of
    return jnp.minimum(jnp.maximum(entries, -bound), bound).astype(held_as)


def setup_inputs(seed: int = 0, part: int = 0) -> dict:
    key_list = jax.random.split(jax.random.key(seed), 21)
    own_keys = jax.random.split(jax.random.fold_in(key_list[20], part), 21)
    video_query = draw_video_query(jax.random.fold_in(jax.random.fold_in(key_list[20], part), 71), part)
    video_key = draw_video_key(jax.random.fold_in(jax.random.fold_in(key_list[20], part), 71), part)
    video_value = centred(own_keys[2], (SAMPLES, LV, DV), 1.0, 6.0, ((1, 16),))
    audio_query = draw_audio_query(jax.random.fold_in(jax.random.fold_in(key_list[20], part), 71), part)
    audio_key = draw_audio_key(jax.random.fold_in(jax.random.fold_in(key_list[20], part), 71), part)
    audio_value = centred(own_keys[5], (SAMPLES, LA, DA), 1.0, 6.0, ((1, 16),))
    cross_audio_query = draw_cross_audio_query(jax.random.fold_in(jax.random.fold_in(key_list[20], part), 71), part)
    cross_video_key = draw_cross_video_key(jax.random.fold_in(jax.random.fold_in(key_list[20], part), 71), part)
    cross_video_value = centred(own_keys[8], (SAMPLES, LV, DA), 1.0, 6.0, ((1, 16),))
    cross_video_query = draw_cross_video_query(jax.random.fold_in(jax.random.fold_in(key_list[20], part), 71), part)
    cross_audio_key = draw_cross_audio_key(jax.random.fold_in(jax.random.fold_in(key_list[20], part), 71), part)
    cross_audio_value = centred(own_keys[11], (SAMPLES, LA, DA), 1.0, 6.0, ((1, 16),))
    audio_frames = place_ends(jax.random.randint(own_keys[12], (SAMPLES, LA), 0, FRAMES), jax.random.fold_in(own_keys[12], 1), 0, FRAMES - 1).astype(jnp.int32)
    into_audio_slope = jnp.clip(jnp.exp(jax.random.uniform(key_list[13], (HA,), jnp.float32, math.log(0.05), math.log(0.5))), 0.05, 0.5)
    into_video_slope = jnp.clip(jnp.exp(jax.random.uniform(key_list[14], (HA,), jnp.float32, math.log(0.05), math.log(0.5))), 0.05, 0.5)
    timestep = jax.random.randint(own_keys[15], (SAMPLES,), 0, TSTEPS).astype(jnp.int32)
    video_gate = jnp.clip(jnp.exp(jax.random.uniform(key_list[16], (TSTEPS, DV), jnp.float32, math.log(2.0), math.log(12.0))), 2.0, 12.0).astype(jnp.bfloat16)
    audio_gate = jnp.clip(jnp.exp(jax.random.uniform(key_list[17], (TSTEPS, DA), jnp.float32, math.log(2.0), math.log(12.0))), 2.0, 12.0).astype(jnp.bfloat16)
    into_audio_gate = jnp.clip(jnp.exp(jax.random.uniform(key_list[18], (TSTEPS, DA), jnp.float32, math.log(2.0), math.log(12.0))), 2.0, 12.0).astype(jnp.bfloat16)
    into_video_gate = jnp.clip(jnp.exp(jax.random.uniform(key_list[19], (TSTEPS, DA), jnp.float32, math.log(2.0), math.log(12.0))), 2.0, 12.0).astype(jnp.bfloat16)
    return dict(video_query=video_query, video_key=video_key, video_value=video_value, audio_query=audio_query, audio_key=audio_key, audio_value=audio_value, cross_audio_query=cross_audio_query, cross_video_key=cross_video_key, cross_video_value=cross_video_value, cross_video_query=cross_video_query, cross_audio_key=cross_audio_key, cross_audio_value=cross_audio_value, audio_frames=audio_frames, into_audio_slope=into_audio_slope, into_video_slope=into_video_slope, timestep=timestep, video_gate=video_gate, audio_gate=audio_gate, into_audio_gate=into_audio_gate, into_video_gate=into_video_gate)


def attend_ref(queries, keyed, valued, heads_n, slopes, query_places, key_places):
    samples, counted, columns = queries.shape
    head_width = columns // heads_n
    score_scale = 1.0 / math.sqrt(head_width)

    def by_heads(tensor):
        return tensor.reshape(samples, tensor.shape[1], heads_n, head_width).transpose(2, 0, 1, 3)

    def one_head(packed):
        head_query_slice, head_key_slice, head_value_slice, slope_value = packed
        logit_scores = jnp.einsum('liv,lzv->liz', head_query_slice.astype(jnp.float32), head_key_slice.astype(jnp.float32)) * score_scale
        logit_scores = logit_scores - slope_value * jnp.abs(query_places[:, :, None] - key_places[:, None, :])
        maxima = lax.optimization_barrier(jnp.max(logit_scores, axis=2))
        exps = jnp.exp(logit_scores - maxima[:, :, None])
        totals = lax.optimization_barrier(jnp.sum(exps, axis=2))
        softmax_weights = exps.astype(jnp.bfloat16).astype(jnp.float32)
        weighted_sum = jnp.einsum('xpr,xre->xpe', softmax_weights, head_value_slice.astype(jnp.float32))
        return weighted_sum / totals[:, :, None]
    result = lax.map(one_head, (by_heads(queries), by_heads(keyed), by_heads(valued), slopes))
    return result.transpose(1, 2, 0, 3).reshape(samples, counted, columns)

def reference(video_query, video_key, video_value, audio_query, audio_key, audio_value, cross_audio_query, cross_video_key, cross_video_value, cross_video_query, cross_audio_key, cross_audio_value, audio_frames, into_audio_slope, into_video_slope, timestep, video_gate, audio_gate, into_audio_gate, into_video_gate):
    frame_of = (jnp.arange(LV, dtype=jnp.int32) // (LV // FRAMES)).astype(jnp.float32)
    video_time = jnp.broadcast_to(frame_of[None, :], (SAMPLES, LV))
    audio_time = audio_frames.astype(jnp.float32)
    still_video = jnp.zeros((SAMPLES, LV), jnp.float32)
    still_audio = jnp.zeros((SAMPLES, LA), jnp.float32)

    def gated(attended, table):
        factor = table[timestep].astype(jnp.float32)
        return (attended * factor[:, None, :]).astype(jnp.bfloat16)
    video_self = gated(attend_ref(video_query, video_key, video_value, HV, jnp.zeros((HV,), jnp.float32), still_video, still_video), video_gate)
    audio_self = gated(attend_ref(audio_query, audio_key, audio_value, HA, jnp.zeros((HA,), jnp.float32), still_audio, still_audio), audio_gate)
    audio_cross = gated(attend_ref(cross_audio_query, cross_video_key, cross_video_value, HA, into_audio_slope, audio_time, video_time), into_audio_gate)
    video_cross = gated(attend_ref(cross_video_query, cross_audio_key, cross_audio_value, HA, into_video_slope, video_time, audio_time), into_video_gate)
    return (video_self, audio_self, audio_cross, video_cross)
```

```python
import functools
import math

import jax
import jax.numpy as jnp
from jax import lax
from jax.experimental import pallas as pl
from jax.experimental.pallas import tpu as pltpu
from jax.sharding import PartitionSpec as P

LV = 4096
FRAMES = 16
DHV = 128
DHA = 64


def partner(value, axis, stride):
    mask = 2**stride
    pairs = [(source, source ^ mask) for source in range(lax.axis_size(axis))]
    return lax.ppermute(value, axis, pairs)


def split_heads(tensor, head_width):
    samples, counted, columns = tensor.shape
    heads_here = columns // head_width
    return (
        tensor.reshape(samples, counted, heads_here, head_width)
        .transpose(0, 2, 1, 3)
        .reshape(samples * heads_here, counted, head_width)
    )


def join_heads(tensor, samples):
    folded, counted, head_width = tensor.shape
    heads_here = folded // samples
    return (
        tensor.reshape(samples, heads_here, counted, head_width)
        .transpose(0, 2, 1, 3)
        .reshape(samples, counted, heads_here * head_width)
    )


def spread(places, samples, heads_here):
    if places.ndim == 1:
        places = places[None, :]
    counted = places.shape[1]
    return jnp.broadcast_to(places[:, None, :], (samples, heads_here, counted)).reshape(
        samples * heads_here, counted
    )


def lane_rows(which_lane, counted, tok_count, head_count):
    tok_ids = jnp.arange(tok_count, dtype=jnp.int32)[:, None]
    return (tok_ids * head_count + which_lane) * counted + jnp.arange(counted, dtype=jnp.int32)[
        None, :
    ]


def key_order(my_lane, other_lane, counted, tok_count, head_count):
    own_rows = lane_rows(my_lane, counted, tok_count, head_count)
    their_rows = lane_rows(other_lane, counted, tok_count, head_count)
    return jnp.concatenate((own_rows.reshape(-1), their_rows.reshape(-1)))


def attend(queries, keyed, valued, slopes, query_places, key_places):
    folded, counted, head_width = queries.shape
    block_rows = math.gcd(counted, 512)
    blocks_count = counted // block_rows
    score_scale = 1.0 / math.sqrt(head_width)
    query_blocks = queries.reshape(folded, blocks_count, block_rows, head_width).transpose(
        1, 0, 2, 3
    )
    place_blocks = query_places.reshape(folded, blocks_count, block_rows).transpose(1, 0, 2)

    def one_block(packed):
        query_block, place_block = packed
        logit_scores = (
            jnp.einsum("fqd,fkd->fqk", query_block, keyed, preferred_element_type=jnp.float32)
            * score_scale
        )
        if slopes is not None:
            logit_scores = logit_scores - slopes[:, None, None] * jnp.abs(
                place_block[:, :, None] - key_places[:, None, :]
            )
        maxima = jnp.max(logit_scores, axis=2)
        exps = jnp.exp(logit_scores - maxima[:, :, None])
        totals = jnp.sum(exps, axis=2)
        weighted_sum = jnp.einsum(
            "fqk,fkd->fqd", exps.astype(jnp.bfloat16), valued, preferred_element_type=jnp.float32
        )
        return (weighted_sum, maxima, totals)

    weighted_sum, maxima, totals = lax.map(one_block, (query_blocks, place_blocks))
    return (
        weighted_sum.transpose(1, 0, 2, 3).reshape(folded, counted, head_width),
        maxima.transpose(1, 0, 2).reshape(folded, counted),
        totals.transpose(1, 0, 2).reshape(folded, counted),
    )


def finish(partials, gate_values, samples):
    weighted_sum, maxima, totals = partials
    gated = weighted_sum / totals[:, :, None] * gate_values
    return join_heads(gated.astype(jnp.bfloat16), samples)


def by_collectives(
    video_query,
    video_key,
    video_value,
    audio_query,
    audio_key,
    audio_value,
    cross_audio_query,
    cross_video_key,
    cross_video_value,
    cross_video_query,
    cross_audio_key,
    cross_audio_value,
    audio_frames,
    into_audio_slope,
    into_video_slope,
    timestep,
    video_gate,
    audio_gate,
    into_audio_gate,
    into_video_gate,
):
    samples, video_rows, video_columns = video_query.shape
    audio_rows = audio_query.shape[1]
    tok_count = lax.axis_size("tok")
    head_count = lax.axis_size("head")
    my_lane = lax.axis_index("head")
    other_lane = 1 - my_lane
    head_first = lax.axis_index("tok")
    patches = LV // FRAMES
    audio_times = lax.all_gather(audio_frames, ("tok", "head"), axis=1, tiled=True).astype(
        jnp.float32
    )
    levels = jnp.arange(video_gate.shape[0], dtype=jnp.int32)
    picker = (timestep[:, None] == levels[None, :]).astype(jnp.bfloat16)

    def video_places(row_ids):
        return (row_ids // patches).astype(jnp.float32)

    def audio_places(row_ids):
        return jnp.take(audio_times, row_ids, axis=1)

    def gate_columns(table, head_width, heads_here):
        row_values = jnp.dot(picker, table, preferred_element_type=jnp.float32)
        picked = lax.dynamic_slice_in_dim(
            row_values, head_first * heads_here * head_width, heads_here * head_width, 1
        )
        return picked.reshape(samples * heads_here, 1, head_width)

    def slope_columns(table, heads_here):
        picked = lax.dynamic_slice_in_dim(table, head_first * heads_here, heads_here, 0)
        return picked[None, :].reshape(-1)

    own_video = lane_rows(my_lane, video_rows, tok_count, head_count).reshape(-1)
    own_audio = lane_rows(my_lane, audio_rows, tok_count, head_count).reshape(-1)
    moved = (
        lax.all_to_all(video_query, "tok", split_axis=2, concat_axis=1, tiled=True),
        lax.all_to_all(video_key, "tok", split_axis=2, concat_axis=1, tiled=True),
        lax.all_to_all(video_value, "tok", split_axis=2, concat_axis=1, tiled=True),
        lax.all_to_all(audio_query, "tok", split_axis=2, concat_axis=1, tiled=True),
        lax.all_to_all(audio_key, "tok", split_axis=2, concat_axis=1, tiled=True),
        lax.all_to_all(audio_value, "tok", split_axis=2, concat_axis=1, tiled=True),
        lax.all_to_all(cross_audio_query, "tok", split_axis=2, concat_axis=1, tiled=True),
        lax.all_to_all(cross_video_key, "tok", split_axis=2, concat_axis=1, tiled=True),
        lax.all_to_all(cross_video_value, "tok", split_axis=2, concat_axis=1, tiled=True),
        lax.all_to_all(cross_video_query, "tok", split_axis=2, concat_axis=1, tiled=True),
        lax.all_to_all(cross_audio_key, "tok", split_axis=2, concat_axis=1, tiled=True),
        lax.all_to_all(cross_audio_value, "tok", split_axis=2, concat_axis=1, tiled=True),
    )
    (
        moved_video_query,
        moved_video_key,
        moved_video_value,
        moved_audio_query,
        moved_audio_key,
        moved_audio_value,
        moved_cross_audio_query,
        moved_cross_video_key,
        moved_cross_video_value,
        moved_cross_video_query,
        moved_cross_audio_key,
        moved_cross_audio_value,
    ) = moved
    partner_pieces = partner(
        (
            moved_video_key,
            moved_video_value,
            moved_audio_key,
            moved_audio_value,
            moved_cross_audio_key,
            moved_cross_audio_value,
            moved_cross_audio_query,
        ),
        "head",
        0,
    )
    full_video_key = jnp.concatenate((moved_video_key, partner_pieces[0]), axis=1)
    full_video_value = jnp.concatenate((moved_video_value, partner_pieces[1]), axis=1)
    full_audio_key = jnp.concatenate((moved_audio_key, partner_pieces[2]), axis=1)
    full_audio_value = jnp.concatenate((moved_audio_value, partner_pieces[3]), axis=1)
    full_cross_audio_key = jnp.concatenate((moved_cross_audio_key, partner_pieces[4]), axis=1)
    full_cross_audio_value = jnp.concatenate((moved_cross_audio_value, partner_pieces[5]), axis=1)
    partner_query = partner_pieces[6]
    video_heads = moved_video_query.shape[2] // DHV
    audio_heads = moved_audio_query.shape[2] // DHA
    audio_key_rows = key_order(my_lane, other_lane, audio_rows, tok_count, head_count)
    still_video = jnp.zeros((samples * video_heads, own_video.shape[0]), jnp.float32)
    still_audio = jnp.zeros((samples * audio_heads, own_audio.shape[0]), jnp.float32)
    video_self = finish(
        attend(
            split_heads(moved_video_query, DHV),
            split_heads(full_video_key, DHV),
            split_heads(full_video_value, DHV),
            None,
            still_video,
            None,
        ),
        gate_columns(video_gate, DHV, video_heads),
        samples,
    )
    audio_self = finish(
        attend(
            split_heads(moved_audio_query, DHA),
            split_heads(full_audio_key, DHA),
            split_heads(full_audio_value, DHA),
            None,
            still_audio,
            None,
        ),
        gate_columns(audio_gate, DHA, audio_heads),
        samples,
    )
    video_slopes = slope_columns(into_video_slope, audio_heads)
    video_cross = finish(
        attend(
            split_heads(moved_cross_video_query, DHA),
            split_heads(full_cross_audio_key, DHA),
            split_heads(full_cross_audio_value, DHA),
            video_slopes,
            spread(video_places(own_video), samples, audio_heads),
            spread(audio_places(audio_key_rows), samples, audio_heads),
        ),
        gate_columns(into_video_gate, DHA, audio_heads),
        samples,
    )
    audio_slopes = slope_columns(into_audio_slope, audio_heads)
    own_audio_places = spread(audio_places(own_audio), samples, audio_heads)
    own_keys = split_heads(moved_cross_video_key, DHA)
    own_values = split_heads(moved_cross_video_value, DHA)
    own_key_places = spread(video_places(own_video), samples, audio_heads)
    own_part = attend(
        split_heads(moved_cross_audio_query, DHA),
        own_keys,
        own_values,
        audio_slopes,
        own_audio_places,
        own_key_places,
    )
    partner_audio = lane_rows(other_lane, audio_rows, tok_count, head_count).reshape(-1)
    their_part = attend(
        split_heads(partner_query, DHA),
        own_keys,
        own_values,
        audio_slopes,
        spread(audio_places(partner_audio), samples, audio_heads),
        own_key_places,
    )
    returned = partner((their_part[0], their_part[1], their_part[2]), "head", 0)
    maxima = jnp.maximum(own_part[1], returned[1])
    own_factor = jnp.exp(own_part[1] - maxima)
    their_factor = jnp.exp(returned[1] - maxima)
    merged = (
        own_part[0] * own_factor[:, :, None] + returned[0] * their_factor[:, :, None],
        maxima,
        own_part[2] * own_factor + returned[2] * their_factor,
    )
    audio_cross = finish(merged, gate_columns(into_audio_gate, DHA, audio_heads), samples)
    return (
        lax.all_to_all(video_self, "tok", split_axis=1, concat_axis=2, tiled=True),
        lax.all_to_all(audio_self, "tok", split_axis=1, concat_axis=2, tiled=True),
        lax.all_to_all(audio_cross, "tok", split_axis=1, concat_axis=2, tiled=True),
        lax.all_to_all(video_cross, "tok", split_axis=1, concat_axis=2, tiled=True),
    )


LANES = 128
LOG2E = 1.4426950408889634
MESH = pl.DeviceIdType.MESH


def softmax_rows(queries, keyed, valued, bias, factor):
    scores = lax.dot_general(
        queries, keyed, (((1,), (1,)), ((), ())), preferred_element_type=jnp.float32
    )
    if bias is not None:
        scores = scores - bias
    maxima = jnp.max(scores, axis=1, keepdims=True)
    exps = jnp.exp2((scores - maxima) * factor)
    totals = jnp.sum(exps, axis=1, keepdims=True)
    summed = jnp.dot(exps.astype(jnp.bfloat16), valued, preferred_element_type=jnp.float32)
    return summed / totals


def kernel(
    hc, n,
    vq, vk, vv, aq, ak, av, caq, cvk, cvv, cvq, cak, cav, fr,
    slope_a, slope_v, gate_v, gate_a, gate_ia, gate_iv,
    out_vs, out_as, out_ac, out_vc,
    vqb, vkb, vvb, vob, aqb, akb, avb, aob, caqb, cvkb, cvvb, caob,
    cvqb, cakb, cavb, cvob, frb, frt,
    vsend, vrecv, xsend, xrecv, fsend, frecv, vosend, xosend, orecv,
):
    me = lax.axis_index("tok") * hc + lax.axis_index("head")
    rows = vq.shape[1]
    arows = aq.shape[1]
    vheads = vqb.shape[0]
    lv = rows * n
    la = arows * n
    patches = lv // FRAMES

    def where(i):
        return {"tok": i // hc, "head": lax.rem(i, hc)}

    def put(src, dst, send_sem, recv_sem, i):
        pltpu.make_async_remote_copy(
            src_ref=src, dst_ref=dst, send_sem=send_sem, recv_sem=recv_sem,
            device_id=where(i), device_id_type=MESH,
        ).start()

    def keep(src, dst, sem):
        pltpu.make_async_copy(src, dst, sem).start()

    def arrived(ref, sem):
        pltpu.make_async_copy(ref, ref, sem).wait()

    def columns(i, which, each):
        return pl.ds(pl.multiple_of((i * each + which) * LANES, LANES), LANES)

    vrows = pl.ds(pl.multiple_of(me * rows, rows), rows)
    myarows = pl.ds(pl.multiple_of(me * arows, arows), arows)

    video = ((vq, vqb), (vk, vkb), (vv, vvb))
    narrow = (
        (cvq, cvqb, vrows), (cak, cakb, myarows), (cav, cavb, myarows),
        (caq, caqb, myarows), (cvk, cvkb, vrows), (cvv, cvvb, vrows),
        (aq, aqb, myarows), (ak, akb, myarows), (av, avb, myarows),
    )

    barrier = pltpu.get_barrier_semaphore()

    def greet(j, carry):
        pl.semaphore_signal(
            barrier, inc=1, device_id=where(lax.rem(me + j, n)), device_id_type=MESH
        )
        return carry

    lax.fori_loop(1, n, greet, 0)

    for h in range(vheads):
        for at, (src, dst) in enumerate(video):
            keep(src.at[0, :, columns(me, h, vheads)], dst.at[h, vrows, :], vrecv.at[h, at])
    for at, (src, dst, here) in enumerate(narrow):
        keep(src.at[0, :, columns(me, 0, 1)], dst.at[here, :], xrecv.at[at])
    keep(fr, frb.at[myarows, :], frecv)

    pl.semaphore_wait(barrier, n - 1)

    for h in range(vheads):

        def send_video(j, carry):
            i = lax.rem(me + j, n)
            for at, (src, dst) in enumerate(video):
                put(
                    src.at[0, :, columns(i, h, vheads)], dst.at[h, vrows, :],
                    vsend.at[h, at], vrecv.at[h, at], i,
                )
            return carry

        lax.fori_loop(1, n, send_video, 0)

    def send_narrow(first, last):
        def body(j, carry):
            i = lax.rem(me + j, n)
            for at in range(first, last):
                src, dst, here = narrow[at]
                put(
                    src.at[0, :, columns(i, 0, 1)], dst.at[here, :],
                    xsend.at[at], xrecv.at[at], i,
                )
            return carry

        lax.fori_loop(1, n, body, 0)

    def send_frames(j, carry):
        i = lax.rem(me + j, n)
        put(fr, frb.at[myarows, :], fsend, frecv, i)
        return carry

    def give(buffer, here, out, cols, send_sem, recv_sem, i):
        @pl.when(i != me)
        def _():
            put(buffer.at[here, :], out.at[0, :, cols], send_sem, recv_sem, i)

        @pl.when(i == me)
        def _():
            keep(buffer.at[here, :], out.at[0, :, cols], recv_sem)

    video_factor = LOG2E / math.sqrt(DHV)
    root = math.sqrt(DHA)
    narrow_factor = LOG2E / root

    for h in range(vheads):
        for at, (_, dst) in enumerate(video):
            arrived(dst.at[h], vrecv.at[h, at])
        if h == 0:
            send_narrow(0, 3)
            lax.fori_loop(1, n, send_frames, 0)
            send_narrow(3, 9)

        def video_block(j, carry):
            i = lax.rem(me + 1 + j, n)
            here = pl.ds(pl.multiple_of(i * rows, rows), rows)
            part = softmax_rows(vqb[h, here, :], vkb[h], vvb[h], None, video_factor)
            gated = part * gate_v[:, h * LANES : (h + 1) * LANES]
            vob[h, here, :] = gated.astype(jnp.bfloat16)
            give(vob.at[h], here, out_vs, columns(me, h, vheads), vosend.at[h], orecv.at[0], i)
            return carry

        lax.fori_loop(0, n, video_block, 0)

    lane = lax.broadcasted_iota(jnp.int32, (1, LANES), 1)
    in_head = [(lane // DHA == h).astype(jnp.float32) for h in range(LANES // DHA)]
    masks = [mask.astype(jnp.bfloat16) for mask in in_head]

    def both_heads(queries, keyed, valued, biases, gate):
        total = None
        for h, mask in enumerate(masks):
            part = softmax_rows(
                queries * mask, keyed, valued, biases(h), narrow_factor
            ) * in_head[h]
            total = part if total is None else total + part
        return (total * gate).astype(jnp.bfloat16)

    arrived(frb, frecv)
    frt[...] = jnp.transpose(frb[...])[0 : frt.shape[0], :]

    for at in range(0, 3):
        arrived(narrow[at][1], xrecv.at[at])

    def video_cross_block(j, carry):
        i = lax.rem(me + 1 + j, n)
        here = pl.ds(pl.multiple_of(i * rows, rows), rows)
        if patches % rows == 0:
            places = (i * rows // patches).astype(jnp.float32)
        else:
            ids = i * rows + lax.broadcasted_iota(jnp.int32, (rows, 1), 0)
            places = (ids // patches).astype(jnp.float32)
        apart = jnp.abs(frt[0:1, :] - places)
        cvob[here, :] = both_heads(
            cvqb[here, :], cakb[...], cavb[...], lambda h: apart * (slope_v[h] * root), gate_iv[...]
        )
        give(cvob, here, out_vc, columns(me, 0, 1), xosend.at[0], orecv.at[1], i)
        return carry

    lax.fori_loop(0, n, video_cross_block, 0)

    block = math.gcd(la, 256)

    def give_audio(buffer, out, send_sem, recv_sem):
        def body(j, carry):
            i = lax.rem(me + 1 + j, n)
            here = pl.ds(pl.multiple_of(i * arows, arows), arows)
            give(buffer, here, out, columns(me, 0, 1), send_sem, recv_sem, i)
            return carry

        lax.fori_loop(0, n, body, 0)

    for at in range(3, 6):
        arrived(narrow[at][1], xrecv.at[at])

    def audio_cross_block(b, carry):
        here = pl.ds(pl.multiple_of(b * block, block), block)
        key_places = (lax.broadcasted_iota(jnp.int32, (1, lv), 1) // patches).astype(jnp.float32)
        apart = jnp.abs(frb[here, 0:1] - key_places)
        caob[here, :] = both_heads(
            caqb[here, :], cvkb[...], cvvb[...], lambda h: apart * (slope_a[h] * root), gate_ia[...]
        )
        return carry

    lax.fori_loop(0, la // block, audio_cross_block, 0)
    give_audio(caob, out_ac, xosend.at[1], orecv.at[2])

    for at in range(6, 9):
        arrived(narrow[at][1], xrecv.at[at])

    def audio_self_block(b, carry):
        here = pl.ds(pl.multiple_of(b * block, block), block)
        aob[here, :] = both_heads(aqb[here, :], akb[...], avb[...], lambda h: None, gate_a[...])
        return carry

    lax.fori_loop(0, la // block, audio_self_block, 0)
    give_audio(aob, out_as, xosend.at[2], orecv.at[3])

    others = n - 1
    for h in range(vheads):
        for at, (src, _) in enumerate(video):
            arrived(src.at[0, :, pl.ds(0, others * LANES)], vsend.at[h, at])
        arrived(vob.at[h, pl.ds(0, others * rows), :], vosend.at[h])
    for at, (src, _, _) in enumerate(narrow):
        arrived(src.at[0, :, pl.ds(0, others * LANES)], xsend.at[at])
    arrived(frb.at[pl.ds(0, others * arows), :], fsend)
    arrived(cvob.at[pl.ds(0, others * rows), :], xosend.at[0])
    arrived(caob.at[pl.ds(0, others * arows), :], xosend.at[1])
    arrived(aob.at[pl.ds(0, others * arows), :], xosend.at[2])
    arrived(out_vs, orecv.at[0])
    arrived(out_vc, orecv.at[1])
    arrived(out_ac, orecv.at[2])
    arrived(out_as, orecv.at[3])


def in_kernel(arguments):
    (
        vq, vk, vv, aq, ak, av, caq, cvk, cvv, cvq, cak, cav, frames,
        audio_slopes, video_slopes, timestep, gv, ga, gia, giv,
    ) = arguments
    hc = lax.axis_size("head")
    n = lax.axis_size("tok") * hc
    me = lax.axis_index("tok") * hc + lax.axis_index("head")
    rows, arows = vq.shape[1], aq.shape[1]
    lv, la = rows * n, arows * n
    vheads = vq.shape[2] // n // LANES
    heads_here = LANES // DHA

    def gate(table, width):
        return lax.dynamic_slice(table, (timestep[0], me * width), (1, width)).astype(jnp.float32)

    def slopes(table):
        return lax.dynamic_slice(table, (me * heads_here,), (heads_here,))

    fr = jnp.broadcast_to(frames.reshape(arows, 1).astype(jnp.float32), (arows, LANES))
    anywhere = pl.BlockSpec(memory_space=pl.ANY)
    in_smem = pl.BlockSpec(memory_space=pltpu.SMEM)
    in_vmem = pl.BlockSpec(memory_space=pltpu.VMEM)

    def held(*shape):
        return pltpu.VMEM(shape, jnp.bfloat16)

    wide, long, short = held(vheads, lv, LANES), held(lv, LANES), held(la, LANES)
    dma = pltpu.SemaphoreType.DMA
    video_self, audio_self, audio_cross, video_cross = pl.pallas_call(
        functools.partial(kernel, hc, n),
        out_shape=[
            jax.ShapeDtypeStruct(vq.shape, jnp.bfloat16),
            jax.ShapeDtypeStruct(aq.shape, jnp.bfloat16),
            jax.ShapeDtypeStruct(caq.shape, jnp.bfloat16),
            jax.ShapeDtypeStruct(cvq.shape, jnp.bfloat16),
        ],
        in_specs=[anywhere] * 13 + [in_smem] * 2 + [in_vmem] * 4,
        out_specs=[anywhere] * 4,
        scratch_shapes=[
            wide, wide, wide, wide,
            short, short, short, short,
            short, long, long, short,
            long, short, short, long,
            pltpu.VMEM((la, LANES), jnp.float32),
            pltpu.VMEM((8, la), jnp.float32),
            dma((vheads, 3)), dma((vheads, 3)), dma((9,)), dma((9,)),
            dma, dma, dma((vheads,)), dma((3,)), dma((4,)),
        ],
        compiler_params=pltpu.CompilerParams(
            collective_id=0, has_side_effects=True, vmem_limit_bytes=56 * 1024 * 1024
        ),
    )(
        vq, vk, vv, aq, ak, av, caq, cvk, cvv, cvq, cak, cav, fr,
        slopes(audio_slopes), slopes(video_slopes),
        gate(gv, vheads * LANES), gate(ga, LANES), gate(gia, LANES), gate(giv, LANES),
    )
    return video_self, audio_self, audio_cross, video_cross


def on_device(*arguments):
    samples, rows, video_columns = arguments[0].shape
    arows, audio_columns = arguments[3].shape[1:]
    n = lax.axis_size("tok") * lax.axis_size("head")
    fits = (
        samples == 1
        and video_columns % (n * DHV) == 0
        and audio_columns == n * LANES
        and rows % 16 == 0
        and arows % 16 == 0
    )
    return in_kernel(arguments) if fits else by_collectives(*arguments)


def solution(mesh):
    placed = (
        P("groups", ("tok", "head"), None),
        P("groups", ("tok", "head"), None),
        P("groups", ("tok", "head"), None),
        P("groups", ("tok", "head"), None),
        P("groups", ("tok", "head"), None),
        P("groups", ("tok", "head"), None),
        P("groups", ("tok", "head"), None),
        P("groups", ("tok", "head"), None),
        P("groups", ("tok", "head"), None),
        P("groups", ("tok", "head"), None),
        P("groups", ("tok", "head"), None),
        P("groups", ("tok", "head"), None),
        P("groups", ("tok", "head")),
        P(),
        P(),
        P("groups"),
        P(),
        P(),
        P(),
        P(),
    )
    return jax.shard_map(
        on_device,
        mesh=mesh,
        in_specs=placed,
        out_specs=(
            P("groups", ("tok", "head"), None),
            P("groups", ("tok", "head"), None),
            P("groups", ("tok", "head"), None),
            P("groups", ("tok", "head"), None),
        ),
        check_vma=False,
    )
```

```python
import functools
import math

import jax
import jax.numpy as jnp
from jax import lax
from jax.experimental import pallas as pl
from jax.experimental.pallas import tpu as pltpu
from jax.sharding import PartitionSpec as P

LV = 4096
FRAMES = 16
DHV = 128
DHA = 64


def partner(value, axis, stride):
    mask = 2**stride
    pairs = [(source, source ^ mask) for source in range(lax.axis_size(axis))]
    return lax.ppermute(value, axis, pairs)


def split_heads(tensor, head_width):
    samples, counted, columns = tensor.shape
    heads_here = columns // head_width
    return (
        tensor.reshape(samples, counted, heads_here, head_width)
        .transpose(0, 2, 1, 3)
        .reshape(samples * heads_here, counted, head_width)
    )


def join_heads(tensor, samples):
    folded, counted, head_width = tensor.shape
    heads_here = folded // samples
    return (
        tensor.reshape(samples, heads_here, counted, head_width)
        .transpose(0, 2, 1, 3)
        .reshape(samples, counted, heads_here * head_width)
    )


def spread(places, samples, heads_here):
    if places.ndim == 1:
        places = places[None, :]
    counted = places.shape[1]
    return jnp.broadcast_to(places[:, None, :], (samples, heads_here, counted)).reshape(
        samples * heads_here, counted
    )


def lane_rows(which_lane, counted, tok_count, head_count):
    tok_ids = jnp.arange(tok_count, dtype=jnp.int32)[:, None]
    return (tok_ids * head_count + which_lane) * counted + jnp.arange(counted, dtype=jnp.int32)[
        None, :
    ]


def key_order(my_lane, other_lane, counted, tok_count, head_count):
    own_rows = lane_rows(my_lane, counted, tok_count, head_count)
    their_rows = lane_rows(other_lane, counted, tok_count, head_count)
    return jnp.concatenate((own_rows.reshape(-1), their_rows.reshape(-1)))


def attend(queries, keyed, valued, slopes, query_places, key_places):
    folded, counted, head_width = queries.shape
    block_rows = math.gcd(counted, 512)
    blocks_count = counted // block_rows
    score_scale = 1.0 / math.sqrt(head_width)
    query_blocks = queries.reshape(folded, blocks_count, block_rows, head_width).transpose(
        1, 0, 2, 3
    )
    place_blocks = query_places.reshape(folded, blocks_count, block_rows).transpose(1, 0, 2)

    def one_block(packed):
        query_block, place_block = packed
        logit_scores = (
            jnp.einsum("fqd,fkd->fqk", query_block, keyed, preferred_element_type=jnp.float32)
            * score_scale
        )
        if slopes is not None:
            logit_scores = logit_scores - slopes[:, None, None] * jnp.abs(
                place_block[:, :, None] - key_places[:, None, :]
            )
        maxima = jnp.max(logit_scores, axis=2)
        exps = jnp.exp(logit_scores - maxima[:, :, None])
        totals = jnp.sum(exps, axis=2)
        weighted_sum = jnp.einsum(
            "fqk,fkd->fqd", exps.astype(jnp.bfloat16), valued, preferred_element_type=jnp.float32
        )
        return (weighted_sum, maxima, totals)

    weighted_sum, maxima, totals = lax.map(one_block, (query_blocks, place_blocks))
    return (
        weighted_sum.transpose(1, 0, 2, 3).reshape(folded, counted, head_width),
        maxima.transpose(1, 0, 2).reshape(folded, counted),
        totals.transpose(1, 0, 2).reshape(folded, counted),
    )


def finish(partials, gate_values, samples):
    weighted_sum, maxima, totals = partials
    gated = weighted_sum / totals[:, :, None] * gate_values
    return join_heads(gated.astype(jnp.bfloat16), samples)


def by_collectives(
    video_query,
    video_key,
    video_value,
    audio_query,
    audio_key,
    audio_value,
    cross_audio_query,
    cross_video_key,
    cross_video_value,
    cross_video_query,
    cross_audio_key,
    cross_audio_value,
    audio_frames,
    into_audio_slope,
    into_video_slope,
    timestep,
    video_gate,
    audio_gate,
    into_audio_gate,
    into_video_gate,
):
    samples, video_rows, video_columns = video_query.shape
    audio_rows = audio_query.shape[1]
    tok_count = lax.axis_size("tok")
    head_count = lax.axis_size("head")
    my_lane = lax.axis_index("head")
    other_lane = 1 - my_lane
    head_first = lax.axis_index("tok")
    patches = LV // FRAMES
    audio_times = lax.all_gather(audio_frames, ("tok", "head"), axis=1, tiled=True).astype(
        jnp.float32
    )
    levels = jnp.arange(video_gate.shape[0], dtype=jnp.int32)
    picker = (timestep[:, None] == levels[None, :]).astype(jnp.bfloat16)

    def video_places(row_ids):
        return (row_ids // patches).astype(jnp.float32)

    def audio_places(row_ids):
        return jnp.take(audio_times, row_ids, axis=1)

    def gate_columns(table, head_width, heads_here):
        row_values = jnp.dot(picker, table, preferred_element_type=jnp.float32)
        picked = lax.dynamic_slice_in_dim(
            row_values, head_first * heads_here * head_width, heads_here * head_width, 1
        )
        return picked.reshape(samples * heads_here, 1, head_width)

    def slope_columns(table, heads_here):
        picked = lax.dynamic_slice_in_dim(table, head_first * heads_here, heads_here, 0)
        return picked[None, :].reshape(-1)

    own_video = lane_rows(my_lane, video_rows, tok_count, head_count).reshape(-1)
    own_audio = lane_rows(my_lane, audio_rows, tok_count, head_count).reshape(-1)
    moved = (
        lax.all_to_all(video_query, "tok", split_axis=2, concat_axis=1, tiled=True),
        lax.all_to_all(video_key, "tok", split_axis=2, concat_axis=1, tiled=True),
        lax.all_to_all(video_value, "tok", split_axis=2, concat_axis=1, tiled=True),
        lax.all_to_all(audio_query, "tok", split_axis=2, concat_axis=1, tiled=True),
        lax.all_to_all(audio_key, "tok", split_axis=2, concat_axis=1, tiled=True),
        lax.all_to_all(audio_value, "tok", split_axis=2, concat_axis=1, tiled=True),
        lax.all_to_all(cross_audio_query, "tok", split_axis=2, concat_axis=1, tiled=True),
        lax.all_to_all(cross_video_key, "tok", split_axis=2, concat_axis=1, tiled=True),
        lax.all_to_all(cross_video_value, "tok", split_axis=2, concat_axis=1, tiled=True),
        lax.all_to_all(cross_video_query, "tok", split_axis=2, concat_axis=1, tiled=True),
        lax.all_to_all(cross_audio_key, "tok", split_axis=2, concat_axis=1, tiled=True),
        lax.all_to_all(cross_audio_value, "tok", split_axis=2, concat_axis=1, tiled=True),
    )
    (
        moved_video_query,
        moved_video_key,
        moved_video_value,
        moved_audio_query,
        moved_audio_key,
        moved_audio_value,
        moved_cross_audio_query,
        moved_cross_video_key,
        moved_cross_video_value,
        moved_cross_video_query,
        moved_cross_audio_key,
        moved_cross_audio_value,
    ) = moved
    partner_pieces = partner(
        (
            moved_video_key,
            moved_video_value,
            moved_audio_key,
            moved_audio_value,
            moved_cross_audio_key,
            moved_cross_audio_value,
            moved_cross_audio_query,
        ),
        "head",
        0,
    )
    full_video_key = jnp.concatenate((moved_video_key, partner_pieces[0]), axis=1)
    full_video_value = jnp.concatenate((moved_video_value, partner_pieces[1]), axis=1)
    full_audio_key = jnp.concatenate((moved_audio_key, partner_pieces[2]), axis=1)
    full_audio_value = jnp.concatenate((moved_audio_value, partner_pieces[3]), axis=1)
    full_cross_audio_key = jnp.concatenate((moved_cross_audio_key, partner_pieces[4]), axis=1)
    full_cross_audio_value = jnp.concatenate((moved_cross_audio_value, partner_pieces[5]), axis=1)
    partner_query = partner_pieces[6]
    video_heads = moved_video_query.shape[2] // DHV
    audio_heads = moved_audio_query.shape[2] // DHA
    audio_key_rows = key_order(my_lane, other_lane, audio_rows, tok_count, head_count)
    still_video = jnp.zeros((samples * video_heads, own_video.shape[0]), jnp.float32)
    still_audio = jnp.zeros((samples * audio_heads, own_audio.shape[0]), jnp.float32)
    video_self = finish(
        attend(
            split_heads(moved_video_query, DHV),
            split_heads(full_video_key, DHV),
            split_heads(full_video_value, DHV),
            None,
            still_video,
            None,
        ),
        gate_columns(video_gate, DHV, video_heads),
        samples,
    )
    audio_self = finish(
        attend(
            split_heads(moved_audio_query, DHA),
            split_heads(full_audio_key, DHA),
            split_heads(full_audio_value, DHA),
            None,
            still_audio,
            None,
        ),
        gate_columns(audio_gate, DHA, audio_heads),
        samples,
    )
    video_slopes = slope_columns(into_video_slope, audio_heads)
    video_cross = finish(
        attend(
            split_heads(moved_cross_video_query, DHA),
            split_heads(full_cross_audio_key, DHA),
            split_heads(full_cross_audio_value, DHA),
            video_slopes,
            spread(video_places(own_video), samples, audio_heads),
            spread(audio_places(audio_key_rows), samples, audio_heads),
        ),
        gate_columns(into_video_gate, DHA, audio_heads),
        samples,
    )
    audio_slopes = slope_columns(into_audio_slope, audio_heads)
    own_audio_places = spread(audio_places(own_audio), samples, audio_heads)
    own_keys = split_heads(moved_cross_video_key, DHA)
    own_values = split_heads(moved_cross_video_value, DHA)
    own_key_places = spread(video_places(own_video), samples, audio_heads)
    own_part = attend(
        split_heads(moved_cross_audio_query, DHA),
        own_keys,
        own_values,
        audio_slopes,
        own_audio_places,
        own_key_places,
    )
    partner_audio = lane_rows(other_lane, audio_rows, tok_count, head_count).reshape(-1)
    their_part = attend(
        split_heads(partner_query, DHA),
        own_keys,
        own_values,
        audio_slopes,
        spread(audio_places(partner_audio), samples, audio_heads),
        own_key_places,
    )
    returned = partner((their_part[0], their_part[1], their_part[2]), "head", 0)
    maxima = jnp.maximum(own_part[1], returned[1])
    own_factor = jnp.exp(own_part[1] - maxima)
    their_factor = jnp.exp(returned[1] - maxima)
    merged = (
        own_part[0] * own_factor[:, :, None] + returned[0] * their_factor[:, :, None],
        maxima,
        own_part[2] * own_factor + returned[2] * their_factor,
    )
    audio_cross = finish(merged, gate_columns(into_audio_gate, DHA, audio_heads), samples)
    return (
        lax.all_to_all(video_self, "tok", split_axis=1, concat_axis=2, tiled=True),
        lax.all_to_all(audio_self, "tok", split_axis=1, concat_axis=2, tiled=True),
        lax.all_to_all(audio_cross, "tok", split_axis=1, concat_axis=2, tiled=True),
        lax.all_to_all(video_cross, "tok", split_axis=1, concat_axis=2, tiled=True),
    )


LANES = 128
LOG2E = 1.4426950408889634
MESH = pl.DeviceIdType.MESH


def softmax_rows(queries, keyed, valued, bias, factor):
    scores = lax.dot_general(
        queries, keyed, (((1,), (1,)), ((), ())), preferred_element_type=jnp.float32
    )
    if bias is not None:
        scores = scores - bias
    maxima = jnp.max(scores, axis=1, keepdims=True)
    exps = jnp.exp2((scores - maxima) * factor)
    totals = jnp.sum(exps, axis=1, keepdims=True)
    summed = jnp.dot(exps.astype(jnp.bfloat16), valued, preferred_element_type=jnp.float32)
    return summed / totals


def kernel(
    hc, n,
    vq, vk, vv, aq, ak, av, caq, cvk, cvv, cvq, cak, cav, fr,
    slope_a, slope_v, level, table_v, table_a, table_ia, table_iv,
    out_vs, out_as, out_ac, out_vc,
    vqb, vkb, vvb, vob, aqb, akb, avb, aob, caqb, cvkb, cvvb, caob,
    cvqb, cakb, cavb, cvob, frb, frt, tvb, tab, tiab, tivb, gvb, gab, giab, givb,
    vsend, vrecv, xsend, xrecv, gsend, grecv, vosend, xosend, orecv, here_sem,
):
    me = lax.axis_index("tok") * hc + lax.axis_index("head")
    rows = vq.shape[1]
    arows = aq.shape[1]
    vheads = vqb.shape[0]
    lv = rows * n
    la = arows * n
    patches = lv // FRAMES

    def where(i):
        return {"tok": i // hc, "head": lax.rem(i, hc)}

    def put(src, dst, send_sem, recv_sem, i):
        pltpu.make_async_remote_copy(
            src_ref=src, dst_ref=dst, send_sem=send_sem, recv_sem=recv_sem,
            device_id=where(i), device_id_type=MESH,
        ).start()

    def keep(src, dst, sem):
        pltpu.make_async_copy(src, dst, sem).start()

    def arrived(ref, sem):
        pltpu.make_async_copy(ref, ref, sem).wait()

    def columns(i, which, each):
        return pl.ds(pl.multiple_of((i * each + which) * LANES, LANES), LANES)

    vrows = pl.ds(pl.multiple_of(me * rows, rows), rows)
    myarows = pl.ds(pl.multiple_of(me * arows, arows), arows)

    video = ((vq, vqb), (vk, vkb), (vv, vvb))
    narrow = (
        (caq, caqb, myarows), (cvk, cvkb, vrows), (cvv, cvvb, vrows),
        (aq, aqb, myarows), (ak, akb, myarows), (av, avb, myarows),
    )

    barrier = pltpu.get_barrier_semaphore()

    def greet(j, carry):
        pl.semaphore_signal(
            barrier, inc=1, device_id=where(lax.rem(me + j, n)), device_id_type=MESH
        )
        return carry

    lax.fori_loop(1, n, greet, 0)

    for h in range(vheads):
        for at, (src, dst) in enumerate(video):
            keep(src.at[0, :, columns(me, h, vheads)], dst.at[h, vrows, :], vrecv.at[h, at])
    for at, (src, dst, here) in enumerate(narrow):
        keep(src.at[0, :, columns(me, 0, 1)], dst.at[here, :], xrecv.at[at])
    tables = ((table_v, tvb, gvb), (table_a, tab, gab), (table_ia, tiab, giab), (table_iv, tivb, givb))
    for at, (src, dst, _) in enumerate(tables):
        width = dst.shape[1]
        first = 0 if width == src.shape[1] else pl.multiple_of(me * width, LANES)
        keep(src.at[:, pl.ds(first, width)], dst, here_sem.at[at])
    keep(cvq.at[0], cvqb, here_sem.at[4])

    ys = 2
    zs = n // hc // ys
    core = lax.axis_index("head")
    yy = lax.rem(lax.axis_index("tok"), ys)
    zz = lax.axis_index("tok") // ys
    shared = ((cak.at[0], cakb), (cav.at[0], cavb), (fr, frb))

    def device(z, y, c):
        return (z * ys + y) * hc + c

    def block_rows(i):
        return pl.ds(pl.multiple_of(i * arows, arows), arows)

    def hand(i, own, slot, target):
        for at, (src, dst) in enumerate(shared):
            held = dst.at[block_rows(i), :]
            put(src if own else held, held, gsend.at[at, slot], grecv.at[at, i], target)

    def got(i):
        for at, (_, dst) in enumerate(shared):
            arrived(dst.at[block_rows(i), :], grecv.at[at, i])

    def up(z, own=False):
        @pl.when(zz < zs - 1)
        def _():
            hand(device(z, yy, core), own, z, device(zz + 1, yy, core))

    def down(z, own=False):
        @pl.when(zz > 0)
        def _():
            hand(device(z, yy, core), own, zs + z, device(zz - 1, yy, core))

    def across(z, own=False):
        hand(device(z, yy, core), own, 2 * zs + z, device(zz, 1 - yy, core))

    def beside(z, y, own=False):
        hand(device(z, y, core), own, 3 * zs + z * ys + y, device(zz, yy, 1 - core))

    for at, (src, dst) in enumerate(shared):
        keep(src, dst.at[block_rows(me), :], grecv.at[at, me])

    pl.semaphore_wait(barrier, n - 1)

    up(zz, True)
    down(zz, True)
    across(zz, True)
    beside(zz, yy, True)

    def send_video(h, first, last):
        def body(j, carry):
            i = lax.rem(me + j, n)
            for at, (src, dst) in enumerate(video):
                put(
                    src.at[0, :, columns(i, h, vheads)], dst.at[h, vrows, :],
                    vsend.at[h, at], vrecv.at[h, at], i,
                )
            return carry

        lax.fori_loop(first, last, body, 0)

    cuts = [1 + (n - 1) * step // (zs + 1) for step in range(zs + 2)]
    send_video(0, cuts[0], cuts[1])
    for s in range(1, zs):

        @pl.when(zz - s >= 0)
        def _():
            got(device(zz - s, yy, core))
            up(zz - s)
            across(zz - s)
            beside(zz - s, yy)

        @pl.when(zz + s < zs)
        def _():
            got(device(zz + s, yy, core))
            down(zz + s)
            across(zz + s)
            beside(zz + s, yy)

        send_video(0, cuts[s], cuts[s + 1])
    send_video(0, cuts[zs], cuts[zs + 1])
    for t in range(zs):
        z = lax.rem(zz + t, zs)
        got(device(z, 1 - yy, core))
        beside(z, 1 - yy)
    for h in range(1, vheads):
        send_video(h, 1, n)
    got(me)
    for t in range(zs):
        for y in range(ys):
            got(device(t, y, 1 - core))

    def send_narrow(first, last):
        def body(j, carry):
            i = lax.rem(me + j, n)
            for at in range(first, last):
                src, dst, here = narrow[at]
                put(
                    src.at[0, :, columns(i, 0, 1)], dst.at[here, :],
                    xsend.at[at], xrecv.at[at], i,
                )
            return carry

        lax.fori_loop(1, n, body, 0)

    def give(buffer, here, out, cols, send_sem, recv_sem, i):
        @pl.when(i != me)
        def _():
            put(buffer.at[here, :], out.at[0, :, cols], send_sem, recv_sem, i)

        @pl.when(i == me)
        def _():
            keep(buffer.at[here, :], out.at[0, :, cols], recv_sem)

    video_factor = LOG2E / math.sqrt(DHV)
    root = math.sqrt(DHA)
    narrow_factor = LOG2E / root

    lane = lax.broadcasted_iota(jnp.int32, (1, LANES), 1)
    in_head = [(lane // DHA == h).astype(jnp.float32) for h in range(LANES // DHA)]
    masks = [mask.astype(jnp.bfloat16) for mask in in_head]

    def both_heads(queries, keyed, valued, biases, gate):
        total = None
        for h, mask in enumerate(masks):
            part = softmax_rows(
                queries * mask, keyed, valued, biases(h), narrow_factor
            ) * in_head[h]
            total = part if total is None else total + part
        return (total * gate).astype(jnp.bfloat16)

    for at, (_, dst, row) in enumerate(tables):
        arrived(dst, here_sem.at[at])
        levels = lax.broadcasted_iota(jnp.int32, (dst.shape[0], 1), 0)
        picked = jnp.where(levels == level[0], dst[...].astype(jnp.float32), 0.0)
        row[0:1, :] = jnp.sum(picked, axis=0, keepdims=True)
    arrived(cvqb, here_sem.at[4])
    frt[...] = jnp.transpose(frb[...])[0 : frt.shape[0], :]
    heads_here = LANES // DHA

    def video_cross_block(p, carry):
        cols = pl.ds(pl.multiple_of(p * LANES, LANES), LANES)
        if patches % rows == 0:
            places = (me * rows // patches).astype(jnp.float32)
        else:
            ids = me * rows + lax.broadcasted_iota(jnp.int32, (rows, 1), 0)
            places = (ids // patches).astype(jnp.float32)
        apart = jnp.abs(frt[0:1, :] - places)
        cvob[:, cols] = both_heads(
            cvqb[:, cols], cakb[:, cols], cavb[:, cols],
            lambda h: apart * (slope_v[p * heads_here + h] * root), givb[0:1, cols],
        )
        return carry

    lax.fori_loop(0, n, video_cross_block, 0)
    keep(cvob, out_vc.at[0], here_sem.at[5])

    for h in range(vheads):
        for at, (_, dst) in enumerate(video):
            arrived(dst.at[h], vrecv.at[h, at])
        if h == 0:
            send_narrow(0, 6)

        def video_block(j, carry):
            i = lax.rem(me + 1 + j, n)
            here = pl.ds(pl.multiple_of(i * rows, rows), rows)
            part = softmax_rows(vqb[h, here, :], vkb[h], vvb[h], None, video_factor)
            gated = part * gvb[0:1, h * LANES : (h + 1) * LANES]
            vob[h, here, :] = gated.astype(jnp.bfloat16)
            give(vob.at[h], here, out_vs, columns(me, h, vheads), vosend.at[h], orecv.at[0], i)
            return carry

        lax.fori_loop(0, n, video_block, 0)

    block = math.gcd(la, 256)

    def give_audio(buffer, out, send_sem, recv_sem):
        def body(j, carry):
            i = lax.rem(me + 1 + j, n)
            here = pl.ds(pl.multiple_of(i * arows, arows), arows)
            give(buffer, here, out, columns(me, 0, 1), send_sem, recv_sem, i)
            return carry

        lax.fori_loop(0, n, body, 0)

    for at in range(0, 3):
        arrived(narrow[at][1], xrecv.at[at])

    def audio_cross_block(b, carry):
        here = pl.ds(pl.multiple_of(b * block, block), block)
        key_places = (lax.broadcasted_iota(jnp.int32, (1, lv), 1) // patches).astype(jnp.float32)
        apart = jnp.abs(frb[here, 0:1] - key_places)
        caob[here, :] = both_heads(
            caqb[here, :], cvkb[...], cvvb[...], lambda h: apart * (slope_a[me * heads_here + h] * root), giab[0:1, :]
        )
        return carry

    lax.fori_loop(0, la // block, audio_cross_block, 0)
    give_audio(caob, out_ac, xosend.at[0], orecv.at[1])

    for at in range(3, 6):
        arrived(narrow[at][1], xrecv.at[at])

    def audio_self_block(b, carry):
        here = pl.ds(pl.multiple_of(b * block, block), block)
        aob[here, :] = both_heads(aqb[here, :], akb[...], avb[...], lambda h: None, gab[0:1, :])
        return carry

    lax.fori_loop(0, la // block, audio_self_block, 0)
    give_audio(aob, out_as, xosend.at[1], orecv.at[2])

    others = n - 1
    for h in range(vheads):
        for at, (src, _) in enumerate(video):
            arrived(src.at[0, :, pl.ds(0, others * LANES)], vsend.at[h, at])
        arrived(vob.at[h, pl.ds(0, others * rows), :], vosend.at[h])
    for at, (src, _, _) in enumerate(narrow):
        arrived(src.at[0, :, pl.ds(0, others * LANES)], xsend.at[at])
    arrived(caob.at[pl.ds(0, others * arows), :], xosend.at[0])
    arrived(aob.at[pl.ds(0, others * arows), :], xosend.at[1])

    def sent(i, slot):
        for at, (_, dst) in enumerate(shared):
            arrived(dst.at[block_rows(i), :], gsend.at[at, slot])

    for z in range(zs):

        @pl.when((z <= zz) & (zz < zs - 1))
        def _():
            sent(device(z, yy, core), z)

        @pl.when((z >= zz) & (zz > 0))
        def _():
            sent(device(z, yy, core), zs + z)

        sent(device(z, yy, core), 2 * zs + z)
        for y in range(ys):
            sent(device(z, y, core), 3 * zs + z * ys + y)
    arrived(out_vs, orecv.at[0])
    arrived(out_ac, orecv.at[1])
    arrived(out_as, orecv.at[2])
    arrived(out_vc.at[0], here_sem.at[5])


def in_kernel(arguments):
    (
        vq, vk, vv, aq, ak, av, caq, cvk, cvv, cvq, cak, cav, frames,
        audio_slopes, video_slopes, timestep, gv, ga, gia, giv,
    ) = arguments
    hc = lax.axis_size("head")
    n = lax.axis_size("tok") * hc
    rows, arows = vq.shape[1], aq.shape[1]
    lv, la = rows * n, arows * n
    vheads = vq.shape[2] // n // LANES
    fr = jnp.broadcast_to(frames.reshape(arows, 1).astype(jnp.float32), (arows, LANES))
    anywhere = pl.BlockSpec(memory_space=pl.ANY)
    in_smem = pl.BlockSpec(memory_space=pltpu.SMEM)

    def held(*shape):
        return pltpu.VMEM(shape, jnp.bfloat16)

    wide, long, short = held(vheads, lv, LANES), held(lv, LANES), held(la, LANES)
    dma = pltpu.SemaphoreType.DMA
    across = aq.shape[2]
    levels = gv.shape[0]
    widths = (vheads * LANES, LANES, LANES, across)
    video_self, audio_self, audio_cross, video_cross = pl.pallas_call(
        functools.partial(kernel, hc, n),
        out_shape=[
            jax.ShapeDtypeStruct(vq.shape, jnp.bfloat16),
            jax.ShapeDtypeStruct(aq.shape, jnp.bfloat16),
            jax.ShapeDtypeStruct(caq.shape, jnp.bfloat16),
            jax.ShapeDtypeStruct(cvq.shape, jnp.bfloat16),
        ],
        in_specs=[anywhere] * 13 + [in_smem] * 3 + [anywhere] * 4,
        out_specs=[anywhere] * 4,
        scratch_shapes=[
            wide, wide, wide, wide,
            short, short, short, short,
            short, long, long, short,
            held(rows, across), held(la, across), held(la, across), held(rows, across),
            pltpu.VMEM((la, LANES), jnp.float32),
            pltpu.VMEM((8, la), jnp.float32),
            *[held(levels, width) for width in widths],
            *[pltpu.VMEM((8, width), jnp.float32) for width in widths],
            dma((vheads, 3)), dma((vheads, 3)), dma((6,)), dma((6,)),
            dma((3, 5 * (n // hc // 2))), dma((3, n)), dma((vheads,)), dma((2,)), dma((3,)), dma((6,)),
        ],
        compiler_params=pltpu.CompilerParams(
            collective_id=0, has_side_effects=True, vmem_limit_bytes=56 * 1024 * 1024
        ),
    )(
        vq, vk, vv, aq, ak, av, caq, cvk, cvv, cvq, cak, cav, fr,
        audio_slopes, video_slopes, timestep, gv, ga, gia, giv,
    )
    return video_self, audio_self, audio_cross, video_cross


def on_device(*arguments):
    samples, rows, video_columns = arguments[0].shape
    arows, audio_columns = arguments[3].shape[1:]
    n = lax.axis_size("tok") * lax.axis_size("head")
    fits = (
        samples == 1
        and lax.axis_size("head") == 2
        and lax.axis_size("tok") % 2 == 0
        and video_columns % (n * DHV) == 0
        and audio_columns == n * LANES
        and rows % 16 == 0
        and arows % 16 == 0
    )
    return in_kernel(arguments) if fits else by_collectives(*arguments)


def solution(mesh):
    placed = (
        P("groups", ("tok", "head"), None),
        P("groups", ("tok", "head"), None),
        P("groups", ("tok", "head"), None),
        P("groups", ("tok", "head"), None),
        P("groups", ("tok", "head"), None),
        P("groups", ("tok", "head"), None),
        P("groups", ("tok", "head"), None),
        P("groups", ("tok", "head"), None),
        P("groups", ("tok", "head"), None),
        P("groups", ("tok", "head"), None),
        P("groups", ("tok", "head"), None),
        P("groups", ("tok", "head"), None),
        P("groups", ("tok", "head")),
        P(),
        P(),
        P("groups"),
        P(),
        P(),
        P(),
        P(),
    )
    return jax.shard_map(
        on_device,
        mesh=mesh,
        in_specs=placed,
        out_specs=(
            P("groups", ("tok", "head"), None),
            P("groups", ("tok", "head"), None),
            P("groups", ("tok", "head"), None),
            P("groups", ("tok", "head"), None),
        ),
        check_vma=False,
    )
```

```python
import functools
import math

import jax
import jax.numpy as jnp
from jax import lax
from jax.experimental import pallas as pl
from jax.experimental.pallas import tpu as pltpu
from jax.sharding import PartitionSpec as P

LV = 4096
FRAMES = 16
DHV = 128
DHA = 64


def partner(value, axis, stride):
    mask = 2**stride
    pairs = [(source, source ^ mask) for source in range(lax.axis_size(axis))]
    return lax.ppermute(value, axis, pairs)


def split_heads(tensor, head_width):
    samples, counted, columns = tensor.shape
    heads_here = columns // head_width
    return (
        tensor.reshape(samples, counted, heads_here, head_width)
        .transpose(0, 2, 1, 3)
        .reshape(samples * heads_here, counted, head_width)
    )


def join_heads(tensor, samples):
    folded, counted, head_width = tensor.shape
    heads_here = folded // samples
    return (
        tensor.reshape(samples, heads_here, counted, head_width)
        .transpose(0, 2, 1, 3)
        .reshape(samples, counted, heads_here * head_width)
    )


def spread(places, samples, heads_here):
    if places.ndim == 1:
        places = places[None, :]
    counted = places.shape[1]
    return jnp.broadcast_to(places[:, None, :], (samples, heads_here, counted)).reshape(
        samples * heads_here, counted
    )


def lane_rows(which_lane, counted, tok_count, head_count):
    tok_ids = jnp.arange(tok_count, dtype=jnp.int32)[:, None]
    return (tok_ids * head_count + which_lane) * counted + jnp.arange(counted, dtype=jnp.int32)[
        None, :
    ]


def key_order(my_lane, other_lane, counted, tok_count, head_count):
    own_rows = lane_rows(my_lane, counted, tok_count, head_count)
    their_rows = lane_rows(other_lane, counted, tok_count, head_count)
    return jnp.concatenate((own_rows.reshape(-1), their_rows.reshape(-1)))


def attend(queries, keyed, valued, slopes, query_places, key_places):
    folded, counted, head_width = queries.shape
    block_rows = math.gcd(counted, 512)
    blocks_count = counted // block_rows
    score_scale = 1.0 / math.sqrt(head_width)
    query_blocks = queries.reshape(folded, blocks_count, block_rows, head_width).transpose(
        1, 0, 2, 3
    )
    place_blocks = query_places.reshape(folded, blocks_count, block_rows).transpose(1, 0, 2)

    def one_block(packed):
        query_block, place_block = packed
        logit_scores = (
            jnp.einsum("fqd,fkd->fqk", query_block, keyed, preferred_element_type=jnp.float32)
            * score_scale
        )
        if slopes is not None:
            logit_scores = logit_scores - slopes[:, None, None] * jnp.abs(
                place_block[:, :, None] - key_places[:, None, :]
            )
        maxima = jnp.max(logit_scores, axis=2)
        exps = jnp.exp(logit_scores - maxima[:, :, None])
        totals = jnp.sum(exps, axis=2)
        weighted_sum = jnp.einsum(
            "fqk,fkd->fqd", exps.astype(jnp.bfloat16), valued, preferred_element_type=jnp.float32
        )
        return (weighted_sum, maxima, totals)

    weighted_sum, maxima, totals = lax.map(one_block, (query_blocks, place_blocks))
    return (
        weighted_sum.transpose(1, 0, 2, 3).reshape(folded, counted, head_width),
        maxima.transpose(1, 0, 2).reshape(folded, counted),
        totals.transpose(1, 0, 2).reshape(folded, counted),
    )


def finish(partials, gate_values, samples):
    weighted_sum, maxima, totals = partials
    gated = weighted_sum / totals[:, :, None] * gate_values
    return join_heads(gated.astype(jnp.bfloat16), samples)


def by_collectives(
    video_query,
    video_key,
    video_value,
    audio_query,
    audio_key,
    audio_value,
    cross_audio_query,
    cross_video_key,
    cross_video_value,
    cross_video_query,
    cross_audio_key,
    cross_audio_value,
    audio_frames,
    into_audio_slope,
    into_video_slope,
    timestep,
    video_gate,
    audio_gate,
    into_audio_gate,
    into_video_gate,
):
    samples, video_rows, video_columns = video_query.shape
    audio_rows = audio_query.shape[1]
    tok_count = lax.axis_size("tok")
    head_count = lax.axis_size("head")
    my_lane = lax.axis_index("head")
    other_lane = 1 - my_lane
    head_first = lax.axis_index("tok")
    patches = LV // FRAMES
    audio_times = lax.all_gather(audio_frames, ("tok", "head"), axis=1, tiled=True).astype(
        jnp.float32
    )
    levels = jnp.arange(video_gate.shape[0], dtype=jnp.int32)
    picker = (timestep[:, None] == levels[None, :]).astype(jnp.bfloat16)

    def video_places(row_ids):
        return (row_ids // patches).astype(jnp.float32)

    def audio_places(row_ids):
        return jnp.take(audio_times, row_ids, axis=1)

    def gate_columns(table, head_width, heads_here):
        row_values = jnp.dot(picker, table, preferred_element_type=jnp.float32)
        picked = lax.dynamic_slice_in_dim(
            row_values, head_first * heads_here * head_width, heads_here * head_width, 1
        )
        return picked.reshape(samples * heads_here, 1, head_width)

    def slope_columns(table, heads_here):
        picked = lax.dynamic_slice_in_dim(table, head_first * heads_here, heads_here, 0)
        return picked[None, :].reshape(-1)

    own_video = lane_rows(my_lane, video_rows, tok_count, head_count).reshape(-1)
    own_audio = lane_rows(my_lane, audio_rows, tok_count, head_count).reshape(-1)
    moved = (
        lax.all_to_all(video_query, "tok", split_axis=2, concat_axis=1, tiled=True),
        lax.all_to_all(video_key, "tok", split_axis=2, concat_axis=1, tiled=True),
        lax.all_to_all(video_value, "tok", split_axis=2, concat_axis=1, tiled=True),
        lax.all_to_all(audio_query, "tok", split_axis=2, concat_axis=1, tiled=True),
        lax.all_to_all(audio_key, "tok", split_axis=2, concat_axis=1, tiled=True),
        lax.all_to_all(audio_value, "tok", split_axis=2, concat_axis=1, tiled=True),
        lax.all_to_all(cross_audio_query, "tok", split_axis=2, concat_axis=1, tiled=True),
        lax.all_to_all(cross_video_key, "tok", split_axis=2, concat_axis=1, tiled=True),
        lax.all_to_all(cross_video_value, "tok", split_axis=2, concat_axis=1, tiled=True),
        lax.all_to_all(cross_video_query, "tok", split_axis=2, concat_axis=1, tiled=True),
        lax.all_to_all(cross_audio_key, "tok", split_axis=2, concat_axis=1, tiled=True),
        lax.all_to_all(cross_audio_value, "tok", split_axis=2, concat_axis=1, tiled=True),
    )
    (
        moved_video_query,
        moved_video_key,
        moved_video_value,
        moved_audio_query,
        moved_audio_key,
        moved_audio_value,
        moved_cross_audio_query,
        moved_cross_video_key,
        moved_cross_video_value,
        moved_cross_video_query,
        moved_cross_audio_key,
        moved_cross_audio_value,
    ) = moved
    partner_pieces = partner(
        (
            moved_video_key,
            moved_video_value,
            moved_audio_key,
            moved_audio_value,
            moved_cross_audio_key,
            moved_cross_audio_value,
            moved_cross_audio_query,
        ),
        "head",
        0,
    )
    full_video_key = jnp.concatenate((moved_video_key, partner_pieces[0]), axis=1)
    full_video_value = jnp.concatenate((moved_video_value, partner_pieces[1]), axis=1)
    full_audio_key = jnp.concatenate((moved_audio_key, partner_pieces[2]), axis=1)
    full_audio_value = jnp.concatenate((moved_audio_value, partner_pieces[3]), axis=1)
    full_cross_audio_key = jnp.concatenate((moved_cross_audio_key, partner_pieces[4]), axis=1)
    full_cross_audio_value = jnp.concatenate((moved_cross_audio_value, partner_pieces[5]), axis=1)
    partner_query = partner_pieces[6]
    video_heads = moved_video_query.shape[2] // DHV
    audio_heads = moved_audio_query.shape[2] // DHA
    audio_key_rows = key_order(my_lane, other_lane, audio_rows, tok_count, head_count)
    still_video = jnp.zeros((samples * video_heads, own_video.shape[0]), jnp.float32)
    still_audio = jnp.zeros((samples * audio_heads, own_audio.shape[0]), jnp.float32)
    video_self = finish(
        attend(
            split_heads(moved_video_query, DHV),
            split_heads(full_video_key, DHV),
            split_heads(full_video_value, DHV),
            None,
            still_video,
            None,
        ),
        gate_columns(video_gate, DHV, video_heads),
        samples,
    )
    audio_self = finish(
        attend(
            split_heads(moved_audio_query, DHA),
            split_heads(full_audio_key, DHA),
            split_heads(full_audio_value, DHA),
            None,
            still_audio,
            None,
        ),
        gate_columns(audio_gate, DHA, audio_heads),
        samples,
    )
    video_slopes = slope_columns(into_video_slope, audio_heads)
    video_cross = finish(
        attend(
            split_heads(moved_cross_video_query, DHA),
            split_heads(full_cross_audio_key, DHA),
            split_heads(full_cross_audio_value, DHA),
            video_slopes,
            spread(video_places(own_video), samples, audio_heads),
            spread(audio_places(audio_key_rows), samples, audio_heads),
        ),
        gate_columns(into_video_gate, DHA, audio_heads),
        samples,
    )
    audio_slopes = slope_columns(into_audio_slope, audio_heads)
    own_audio_places = spread(audio_places(own_audio), samples, audio_heads)
    own_keys = split_heads(moved_cross_video_key, DHA)
    own_values = split_heads(moved_cross_video_value, DHA)
    own_key_places = spread(video_places(own_video), samples, audio_heads)
    own_part = attend(
        split_heads(moved_cross_audio_query, DHA),
        own_keys,
        own_values,
        audio_slopes,
        own_audio_places,
        own_key_places,
    )
    partner_audio = lane_rows(other_lane, audio_rows, tok_count, head_count).reshape(-1)
    their_part = attend(
        split_heads(partner_query, DHA),
        own_keys,
        own_values,
        audio_slopes,
        spread(audio_places(partner_audio), samples, audio_heads),
        own_key_places,
    )
    returned = partner((their_part[0], their_part[1], their_part[2]), "head", 0)
    maxima = jnp.maximum(own_part[1], returned[1])
    own_factor = jnp.exp(own_part[1] - maxima)
    their_factor = jnp.exp(returned[1] - maxima)
    merged = (
        own_part[0] * own_factor[:, :, None] + returned[0] * their_factor[:, :, None],
        maxima,
        own_part[2] * own_factor + returned[2] * their_factor,
    )
    audio_cross = finish(merged, gate_columns(into_audio_gate, DHA, audio_heads), samples)
    return (
        lax.all_to_all(video_self, "tok", split_axis=1, concat_axis=2, tiled=True),
        lax.all_to_all(audio_self, "tok", split_axis=1, concat_axis=2, tiled=True),
        lax.all_to_all(audio_cross, "tok", split_axis=1, concat_axis=2, tiled=True),
        lax.all_to_all(video_cross, "tok", split_axis=1, concat_axis=2, tiled=True),
    )


LANES = 128
LOG2E = 1.4426950408889634
MESH = pl.DeviceIdType.MESH


def softmax_rows(queries, keyed, valued, bias, factor):
    scores = lax.dot_general(
        queries, keyed, (((1,), (1,)), ((), ())), preferred_element_type=jnp.float32
    )
    if bias is not None:
        scores = scores - bias
    maxima = jnp.max(scores, axis=1, keepdims=True)
    exps = jnp.exp2((scores - maxima) * factor)
    totals = jnp.sum(exps, axis=1, keepdims=True)
    summed = jnp.dot(exps.astype(jnp.bfloat16), valued, preferred_element_type=jnp.float32)
    return summed / totals


def kernel(
    hc, n,
    vq, vk, vv, aq, ak, av, caq, cvk, cvv, cvq, cak, cav, fr,
    slope_a, slope_v, level, table_v, table_a, table_ia, table_iv,
    out_vs, out_as, out_ac, out_vc,
    vqb, vkb, vvb, vob, aqb, akb, avb, aob, caqb, cvkb, cvvb, caob,
    cvqb, cakb, cavb, cvob, frb, frt, tvb, tab, tiab, tivb, gvb, gab, giab, givb,
    vsend, vrecv, xsend, xrecv, gsend, grecv, vosend, xosend, orecv, here_sem,
):
    me = lax.axis_index("tok") * hc + lax.axis_index("head")
    rows = vq.shape[1]
    arows = aq.shape[1]
    vheads = vqb.shape[0]
    lv = rows * n
    la = arows * n
    patches = lv // FRAMES

    def where(i):
        return {"tok": i // hc, "head": lax.rem(i, hc)}

    def put(src, dst, send_sem, recv_sem, i):
        pltpu.make_async_remote_copy(
            src_ref=src, dst_ref=dst, send_sem=send_sem, recv_sem=recv_sem,
            device_id=where(i), device_id_type=MESH,
        ).start()

    def keep(src, dst, sem):
        pltpu.make_async_copy(src, dst, sem).start()

    def arrived(ref, sem):
        pltpu.make_async_copy(ref, ref, sem).wait()

    def columns(i, which, each):
        return pl.ds(pl.multiple_of((i * each + which) * LANES, LANES), LANES)

    vrows = pl.ds(pl.multiple_of(me * rows, rows), rows)
    myarows = pl.ds(pl.multiple_of(me * arows, arows), arows)

    video = ((vq, vqb), (vk, vkb), (vv, vvb))
    narrow = (
        (caq, caqb, myarows), (cvk, cvkb, vrows), (cvv, cvvb, vrows),
        (aq, aqb, myarows), (ak, akb, myarows), (av, avb, myarows),
    )

    barrier = pltpu.get_barrier_semaphore()

    def greet(j, carry):
        pl.semaphore_signal(
            barrier, inc=1, device_id=where(lax.rem(me + j, n)), device_id_type=MESH
        )
        return carry

    lax.fori_loop(1, n, greet, 0)

    for h in range(vheads):
        for at, (src, dst) in enumerate(video):
            keep(src.at[0, :, columns(me, h, vheads)], dst.at[h, vrows, :], vrecv.at[h, at])
    for at, (src, dst, here) in enumerate(narrow):
        keep(src.at[0, :, columns(me, 0, 1)], dst.at[here, :], xrecv.at[at])
    tables = ((table_v, tvb, gvb), (table_a, tab, gab), (table_ia, tiab, giab), (table_iv, tivb, givb))
    for at, (src, dst, _) in enumerate(tables):
        width = dst.shape[1]
        first = 0 if width == src.shape[1] else pl.multiple_of(me * width, LANES)
        keep(src.at[:, pl.ds(first, width)], dst, here_sem.at[at])
    keep(cvq.at[0], cvqb, here_sem.at[4])

    ys = 2
    zs = n // hc // ys
    core = lax.axis_index("head")
    yy = lax.rem(lax.axis_index("tok"), ys)
    zz = lax.axis_index("tok") // ys
    shared = ((cak.at[0], cakb), (cav.at[0], cavb), (fr, frb))

    def device(z, y, c):
        return (z * ys + y) * hc + c

    def block_rows(i):
        return pl.ds(pl.multiple_of(i * arows, arows), arows)

    def hand(i, own, slot, target):
        for at, (src, dst) in enumerate(shared):
            held = dst.at[block_rows(i), :]
            put(src if own else held, held, gsend.at[at, slot], grecv.at[at, i], target)

    def got(i):
        for at, (_, dst) in enumerate(shared):
            arrived(dst.at[block_rows(i), :], grecv.at[at, i])

    def up(z, own=False):
        @pl.when(zz < zs - 1)
        def _():
            hand(device(z, yy, core), own, z, device(zz + 1, yy, core))

    def down(z, own=False):
        @pl.when(zz > 0)
        def _():
            hand(device(z, yy, core), own, zs + z, device(zz - 1, yy, core))

    def across(z, own=False):
        hand(device(z, yy, core), own, 2 * zs + z, device(zz, 1 - yy, core))

    def beside(z, y, own=False):
        hand(device(z, y, core), own, 3 * zs + z * ys + y, device(zz, yy, 1 - core))

    for at, (src, dst) in enumerate(shared):
        keep(src, dst.at[block_rows(me), :], grecv.at[at, me])

    pl.semaphore_wait(barrier, n - 1)

    up(zz, True)
    down(zz, True)
    across(zz, True)
    beside(zz, yy, True)

    def send_video(h, first, last):
        def body(j, carry):
            i = lax.rem(me + j, n)
            for at, (src, dst) in enumerate(video):
                put(
                    src.at[0, :, columns(i, h, vheads)], dst.at[h, vrows, :],
                    vsend.at[h, at], vrecv.at[h, at], i,
                )
            return carry

        lax.fori_loop(first, last, body, 0)

    cuts = [1 + (n - 1) * step // (zs + 1) for step in range(zs + 2)]
    send_video(0, cuts[0], cuts[1])
    for s in range(1, zs):

        @pl.when(zz - s >= 0)
        def _():
            got(device(zz - s, yy, core))
            up(zz - s)
            across(zz - s)
            beside(zz - s, yy)

        @pl.when(zz + s < zs)
        def _():
            got(device(zz + s, yy, core))
            down(zz + s)
            across(zz + s)
            beside(zz + s, yy)

        send_video(0, cuts[s], cuts[s + 1])
    send_video(0, cuts[zs], cuts[zs + 1])
    for t in range(zs):
        z = lax.rem(zz + t, zs)
        got(device(z, 1 - yy, core))
        beside(z, 1 - yy)
    for h in range(1, vheads):
        send_video(h, 1, n)
    got(me)
    for t in range(zs):
        for y in range(ys):
            got(device(t, y, 1 - core))

    def send_narrow(first, last):
        def body(j, carry):
            i = lax.rem(me + j, n)
            for at in range(first, last):
                src, dst, here = narrow[at]
                put(
                    src.at[0, :, columns(i, 0, 1)], dst.at[here, :],
                    xsend.at[at], xrecv.at[at], i,
                )
            return carry

        lax.fori_loop(1, n, body, 0)

    def give(buffer, here, out, cols, send_sem, recv_sem, i):
        @pl.when(i != me)
        def _():
            put(buffer.at[here, :], out.at[0, :, cols], send_sem, recv_sem, i)

        @pl.when(i == me)
        def _():
            keep(buffer.at[here, :], out.at[0, :, cols], recv_sem)

    video_factor = LOG2E / math.sqrt(DHV)
    root = math.sqrt(DHA)
    narrow_factor = LOG2E / root

    lane = lax.broadcasted_iota(jnp.int32, (1, LANES), 1)
    in_head = [(lane // DHA == h).astype(jnp.float32) for h in range(LANES // DHA)]
    masks = [mask.astype(jnp.bfloat16) for mask in in_head]

    def both_heads(queries, keyed, valued, biases, gate):
        total = None
        for h, mask in enumerate(masks):
            part = softmax_rows(
                queries * mask, keyed, valued, biases(h), narrow_factor
            ) * in_head[h]
            total = part if total is None else total + part
        return (total * gate).astype(jnp.bfloat16)

    for at, (_, dst, row) in enumerate(tables):
        arrived(dst, here_sem.at[at])
        levels = lax.broadcasted_iota(jnp.int32, (dst.shape[0], 1), 0)
        picked = jnp.where(levels == level[0], dst[...].astype(jnp.float32), 0.0)
        row[0:1, :] = jnp.sum(picked, axis=0, keepdims=True)
    arrived(cvqb, here_sem.at[4])
    frt[...] = jnp.transpose(frb[...])[0 : frt.shape[0], :]
    heads_here = LANES // DHA

    def video_cross_block(p, carry):
        cols = pl.ds(pl.multiple_of(p * LANES, LANES), LANES)
        if patches % rows == 0:
            places = (me * rows // patches).astype(jnp.float32)
        else:
            ids = me * rows + lax.broadcasted_iota(jnp.int32, (rows, 1), 0)
            places = (ids // patches).astype(jnp.float32)
        apart = jnp.abs(frt[0:1, :] - places)
        cvob[:, cols] = both_heads(
            cvqb[:, cols], cakb[:, cols], cavb[:, cols],
            lambda h: apart * (slope_v[p * heads_here + h] * root), givb[0:1, cols],
        )
        return carry

    lax.fori_loop(0, n, video_cross_block, 0)
    keep(cvob, out_vc.at[0], here_sem.at[5])

    for h in range(vheads):
        for at, (_, dst) in enumerate(video):
            arrived(dst.at[h], vrecv.at[h, at])
        if h == 0:
            send_narrow(0, 3)
            send_narrow(3, 6)

        def video_block(j, carry):
            i = lax.rem(me + 1 + j, n)
            here = pl.ds(pl.multiple_of(i * rows, rows), rows)
            part = softmax_rows(vqb[h, here, :], vkb[h], vvb[h], None, video_factor)
            gated = part * gvb[0:1, h * LANES : (h + 1) * LANES]
            vob[h, here, :] = gated.astype(jnp.bfloat16)
            give(vob.at[h], here, out_vs, columns(me, h, vheads), vosend.at[h], orecv.at[0], i)
            return carry

        lax.fori_loop(0, n, video_block, 0)

    block = math.gcd(la, 256)

    def give_audio(buffer, out, send_sem, recv_sem):
        def body(j, carry):
            i = lax.rem(me + 1 + j, n)
            here = pl.ds(pl.multiple_of(i * arows, arows), arows)
            give(buffer, here, out, columns(me, 0, 1), send_sem, recv_sem, i)
            return carry

        lax.fori_loop(0, n, body, 0)

    for at in range(0, 3):
        arrived(narrow[at][1], xrecv.at[at])

    def audio_cross_block(b, carry):
        here = pl.ds(pl.multiple_of(b * block, block), block)
        key_places = (lax.broadcasted_iota(jnp.int32, (1, lv), 1) // patches).astype(jnp.float32)
        apart = jnp.abs(frb[here, 0:1] - key_places)
        caob[here, :] = both_heads(
            caqb[here, :], cvkb[...], cvvb[...], lambda h: apart * (slope_a[me * heads_here + h] * root), giab[0:1, :]
        )
        return carry

    lax.fori_loop(0, la // block, audio_cross_block, 0)
    give_audio(caob, out_ac, xosend.at[0], orecv.at[1])

    for at in range(3, 6):
        arrived(narrow[at][1], xrecv.at[at])

    def audio_self_block(b, carry):
        here = pl.ds(pl.multiple_of(b * block, block), block)
        aob[here, :] = both_heads(aqb[here, :], akb[...], avb[...], lambda h: None, gab[0:1, :])
        return carry

    lax.fori_loop(0, la // block, audio_self_block, 0)
    give_audio(aob, out_as, xosend.at[1], orecv.at[2])

    others = n - 1
    for h in range(vheads):
        for at, (src, _) in enumerate(video):
            arrived(src.at[0, :, pl.ds(0, others * LANES)], vsend.at[h, at])
        arrived(vob.at[h, pl.ds(0, others * rows), :], vosend.at[h])
    for at, (src, _, _) in enumerate(narrow):
        arrived(src.at[0, :, pl.ds(0, others * LANES)], xsend.at[at])
    arrived(caob.at[pl.ds(0, others * arows), :], xosend.at[0])
    arrived(aob.at[pl.ds(0, others * arows), :], xosend.at[1])

    def sent(i, slot):
        for at, (_, dst) in enumerate(shared):
            arrived(dst.at[block_rows(i), :], gsend.at[at, slot])

    for z in range(zs):

        @pl.when((z <= zz) & (zz < zs - 1))
        def _():
            sent(device(z, yy, core), z)

        @pl.when((z >= zz) & (zz > 0))
        def _():
            sent(device(z, yy, core), zs + z)

        sent(device(z, yy, core), 2 * zs + z)
        for y in range(ys):
            sent(device(z, y, core), 3 * zs + z * ys + y)
    arrived(out_vs, orecv.at[0])
    arrived(out_ac, orecv.at[1])
    arrived(out_as, orecv.at[2])
    arrived(out_vc.at[0], here_sem.at[5])


def in_kernel(arguments):
    (
        vq, vk, vv, aq, ak, av, caq, cvk, cvv, cvq, cak, cav, frames,
        audio_slopes, video_slopes, timestep, gv, ga, gia, giv,
    ) = arguments
    hc = lax.axis_size("head")
    n = lax.axis_size("tok") * hc
    rows, arows = vq.shape[1], aq.shape[1]
    lv, la = rows * n, arows * n
    vheads = vq.shape[2] // n // LANES
    fr = jnp.broadcast_to(frames.reshape(arows, 1).astype(jnp.float32), (arows, LANES))
    anywhere = pl.BlockSpec(memory_space=pl.ANY)
    in_smem = pl.BlockSpec(memory_space=pltpu.SMEM)

    def held(*shape):
        return pltpu.VMEM(shape, jnp.bfloat16)

    wide, long, short = held(vheads, lv, LANES), held(lv, LANES), held(la, LANES)
    dma = pltpu.SemaphoreType.DMA
    across = aq.shape[2]
    levels = gv.shape[0]
    widths = (vheads * LANES, LANES, LANES, across)
    video_self, audio_self, audio_cross, video_cross = pl.pallas_call(
        functools.partial(kernel, hc, n),
        out_shape=[
            jax.ShapeDtypeStruct(vq.shape, jnp.bfloat16),
            jax.ShapeDtypeStruct(aq.shape, jnp.bfloat16),
            jax.ShapeDtypeStruct(caq.shape, jnp.bfloat16),
            jax.ShapeDtypeStruct(cvq.shape, jnp.bfloat16),
        ],
        in_specs=[anywhere] * 13 + [in_smem] * 3 + [anywhere] * 4,
        out_specs=[anywhere] * 4,
        scratch_shapes=[
            wide, wide, wide, wide,
            short, short, short, short,
            short, long, long, short,
            held(rows, across), held(la, across), held(la, across), held(rows, across),
            pltpu.VMEM((la, LANES), jnp.float32),
            pltpu.VMEM((8, la), jnp.float32),
            *[held(levels, width) for width in widths],
            *[pltpu.VMEM((8, width), jnp.float32) for width in widths],
            dma((vheads, 3)), dma((vheads, 3)), dma((6,)), dma((6,)),
            dma((3, 5 * (n // hc // 2))), dma((3, n)), dma((vheads,)), dma((2,)), dma((3,)), dma((6,)),
        ],
        compiler_params=pltpu.CompilerParams(
            collective_id=0, has_side_effects=True, vmem_limit_bytes=56 * 1024 * 1024
        ),
    )(
        vq, vk, vv, aq, ak, av, caq, cvk, cvv, cvq, cak, cav, fr,
        audio_slopes, video_slopes, timestep, gv, ga, gia, giv,
    )
    return video_self, audio_self, audio_cross, video_cross


def on_device(*arguments):
    samples, rows, video_columns = arguments[0].shape
    arows, audio_columns = arguments[3].shape[1:]
    n = lax.axis_size("tok") * lax.axis_size("head")
    fits = (
        samples == 1
        and lax.axis_size("head") == 2
        and lax.axis_size("tok") % 2 == 0
        and video_columns % (n * DHV) == 0
        and audio_columns == n * LANES
        and rows % 16 == 0
        and arows % 16 == 0
    )
    return in_kernel(arguments) if fits else by_collectives(*arguments)


def solution(mesh):
    placed = (
        P("groups", ("tok", "head"), None),
        P("groups", ("tok", "head"), None),
        P("groups", ("tok", "head"), None),
        P("groups", ("tok", "head"), None),
        P("groups", ("tok", "head"), None),
        P("groups", ("tok", "head"), None),
        P("groups", ("tok", "head"), None),
        P("groups", ("tok", "head"), None),
        P("groups", ("tok", "head"), None),
        P("groups", ("tok", "head"), None),
        P("groups", ("tok", "head"), None),
        P("groups", ("tok", "head"), None),
        P("groups", ("tok", "head")),
        P(),
        P(),
        P("groups"),
        P(),
        P(),
        P(),
        P(),
    )
    return jax.shard_map(
        on_device,
        mesh=mesh,
        in_specs=placed,
        out_specs=(
            P("groups", ("tok", "head"), None),
            P("groups", ("tok", "head"), None),
            P("groups", ("tok", "head"), None),
            P("groups", ("tok", "head"), None),
        ),
        check_vma=False,
    )
```
